32 devices in a mesh: dp: 4 (over z), expert: 2 (over y), tensor: 4 (over x, core).
Axes of the slice: x: 2, y: 2, z: 4, core: 2. Of those that a mesh axis runs over, the one named last changes fastest.
Arguments:
- tokens: bfloat16 [512, 6144], P(('dp', 'expert', 'tensor')), may hold values from -6 to 6
- expert_ids: int32 [512, 2], P(('dp', 'expert', 'tensor')), may hold values from 0 to 7, all different within a row; in each aligned block of 16 rows (0 to 15, 16 to 31, ...) at most 8 rows name the same one
- gate_values: float32 [512, 2], P(('dp', 'expert', 'tensor')), may hold values from 0.25 to 1
- w_gate: bfloat16 [2, 6144, 8192], P('expert', 'dp', 'tensor'), may hold values from -0.078125 to 0.078125
- w_up: bfloat16 [2, 6144, 8192], P('expert', 'dp', 'tensor'), may hold values from -0.078125 to 0.078125
- w_down: bfloat16 [2, 8192, 6144], P('expert', 'tensor', 'dp'), may hold values from -0.0625 to 0.0625
- grad_out: bfloat16 [512, 6144], P(('dp', 'expert', 'tensor')), may hold values from -6 to 6
Outputs:
- mixed: bfloat16 [512, 6144], P(('dp', 'expert', 'tensor'))
- grad_tokens: bfloat16 [512, 6144], P(('dp', 'expert', 'tensor'))
- grad_gate: float32 [2, 6144, 8192], P('expert', 'dp', 'tensor')
- grad_up: float32 [2, 6144, 8192], P('expert', 'dp', 'tensor')
- grad_down: float32 [2, 8192, 6144], P('expert', 'tensor', 'dp')
The draws below stay inside these ranges and needn't reach their ends.
Inputs may be any that keep to these rules, and one draw needn't show every extreme that they name: `expert_ids`: each row names two different experts; in the rows of one device no expert is named by more than 8 rows.
All inputs are finite; a program needn't handle non-finite values.
Results may differ from the reference program's by a relative error of at most 0.022.
Values may be sent and summed in bfloat16 or wider, within the bound.
A program may use at most 128 MiB of HBM per device.

```python
import math
import jax
import jax.numpy as jnp
import numpy as np
from jax import lax

D = 6144
E_ALL = 8
FF = 8192
TOK_DEV = 16
CAP = 8
EXPERTS = 2
TOKENS = 512
N_TENSOR = 4


def block_scale(key, extent, split, low, largest):
    def one(position, shards_of):
        steps = jax.random.uniform(jax.random.fold_in(jax.random.fold_in(key, 6), position), (shards_of,), jnp.float32, low / len(split), largest / len(split))
        return jnp.repeat(jnp.exp(steps), extent[position] // shards_of).reshape((-1,) + (1,) * (len(extent) - position - 1))

    loudness = one(*split[0])
    for cut in split[1:]:
        loudness = loudness * one(*cut)
    return loudness


def shared_out(rng, own, number, rows, number_of, top, limit, slope):
    ranking = jax.random.permutation(rng, number_of)
    heavy_load, common = portions_of(number_of, rows * top, limit, slope, True), portions_of(number_of, rows * top, limit, slope, False)
    places = jnp.arange(number_of)

    def named(lengths, rotation):
        used = int((lengths > 0).sum())
        fixed = max(1, used // 4)
        shifted = fixed + (places - fixed + rotation * (used - fixed)) % max(1, number_of - fixed)
        return jnp.zeros((number_of,), jnp.int32).at[ranking[jnp.where(places < fixed, places, shifted)]].set(jnp.asarray(lengths, jnp.int32))

    lengths = jnp.where(number % 4 == 0, named(heavy_load, number // 4), named(common, number - number // 4 - 1))
    mixed = jax.random.permutation(jax.random.fold_in(own, 3), number_of)
    giver, receiver = mixed[0:number_of // 2 * 2:2], mixed[1:number_of // 2 * 2:2]
    room = jnp.minimum(lengths[giver] - 1, limit - lengths[receiver]) // 2
    room = jnp.where((giver == ranking[0]) | (receiver == ranking[0]) | (lengths[receiver] == 0), 0, jnp.maximum(room, 0))
    shifted = jax.random.randint(jax.random.fold_in(own, 4), (number_of // 2,), 0, 1 << 20) % (room + 1)
    lengths = lengths.at[giver].add(-shifted).at[receiver].add(shifted)
    members = jnp.searchsorted(jnp.cumsum(lengths), jnp.arange(rows * top), side="right").astype(jnp.int32)
    grid = members.reshape(top, rows).T
    grid = grid[jax.random.permutation(jax.random.fold_in(own, 1), rows)]
    rotation = jax.random.randint(jax.random.fold_in(own, 2), (rows, 1), 0, top)
    return jnp.take_along_axis(grid, (jnp.arange(top)[None, :] + rotation) % top, axis=1)


def portions_of(number_of, total, bound, slope, full):
    weights = [(1 << 20) // math.isqrt(rank ** slope) + 1 for rank in range(1, number_of + 1)]
    largest = bound if full else min(bound, max(-(-total // number_of), total * weights[0] // sum(weights)))
    least = 1 if total - largest >= number_of - 1 else 0
    holding, surplus = [largest] + [least] * (number_of - 1), total - largest - least * (number_of - 1)
    while surplus > 0:
        free = [i for i in range(1, number_of) if holding[i] < largest] or [i for i in range(1, number_of) if holding[i] < bound]
        pool, left = sum([weights[i] for i in free]), surplus
        for i in free:
            addition = min(bound - holding[i], max(1, left * weights[i] // pool), surplus)
            holding[i] = holding[i] + addition
            surplus = surplus - addition
    return np.array(holding)


def scatter_about(key, dims, scale, most, split=(), dtype=jnp.bfloat16):
    entries = jax.random.normal(key, dims, jnp.float32) * scale
    if len(split) > 0:
        entries = block_scale(key, dims, split, -0.22, 0.18) * entries
    return jnp.clip(entries, min=-most, max=most).astype(dtype)


def setup_inputs(seed: int = 0) -> dict:
    key_of = jax.random.split(jax.random.key(seed), 8)
    tokens = scatter_about(key_of[0], (TOKENS, D), 1.0, 6.0, ((0, 32),))
    expert_ids_keys = jax.random.split(jax.random.fold_in(key_of[1], 1), TOKENS // TOK_DEV)
    expert_ids_turns = jax.random.permutation(jax.random.fold_in(key_of[1], 3), TOKENS // TOK_DEV)
    expert_ids = jax.vmap(lambda own, number: shared_out(jax.random.fold_in(key_of[1], 2), own, number, TOK_DEV, E_ALL, 2, CAP, 2))(expert_ids_keys, expert_ids_turns).reshape((TOKENS, 2))
    gate_values = jnp.clip(0.25 + 0.75 * jax.random.uniform(key_of[2], (TOKENS, 2), jnp.float32) ** block_scale(key_of[2], (TOKENS, 2), ((0, 32),), -0.2, 0.2), 0.25, 1.0)
    w_gate = scatter_about(key_of[3], (EXPERTS, D, FF), D ** -0.5, 0.078125, ((0, 2), (1, 4), (2, 4)))
    w_up = scatter_about(key_of[4], (EXPERTS, D, FF), D ** -0.5, 0.078125, ((0, 2), (1, 4), (2, 4)))
    w_down = scatter_about(key_of[5], (EXPERTS, FF, D), FF ** -0.5, 0.0625, ((0, 2), (1, 4), (2, 4)))
    grad_out = scatter_about(key_of[6], (TOKENS, D), 1.0, 6.0, ((0, 32),))
    return dict(tokens=tokens, expert_ids=expert_ids, gate_values=gate_values, w_gate=w_gate, w_up=w_up, w_down=w_down, grad_out=grad_out)


def blockwise(left, right):
    width = left.shape[1] // N_TENSOR
    total = jnp.zeros((left.shape[0], right.shape[1]), jnp.float32)
    for block in range(N_TENSOR):
        term = jnp.dot(left[:, block * width:(block + 1) * width], right[block * width:(block + 1) * width, :], preferred_element_type=jnp.float32)
        term = lax.optimization_barrier(term.astype(jnp.bfloat16))
        total = total + term.astype(jnp.float32)
    return total.astype(jnp.bfloat16)


def reference(tokens, expert_ids, gate_values, w_gate, w_up, w_down, grad_out):
    mixed = jnp.zeros(tokens.shape, jnp.float32)
    grad_tokens = jnp.zeros(tokens.shape, jnp.float32)
    gate_list = []
    up_list = []
    down_list = []
    for expert in range(EXPERTS):
        chosen = (expert_ids == expert).astype(jnp.float32)
        weight = jnp.sum(gate_values * chosen, axis=1)
        picked = jnp.sum(chosen, axis=1)
        gate = jnp.dot(tokens, w_gate[expert], preferred_element_type=jnp.float32)
        upper = jnp.dot(tokens, w_up[expert], preferred_element_type=jnp.float32)
        sigma = jax.nn.sigmoid(gate)
        active = gate * sigma
        hidden = (active * upper).astype(jnp.bfloat16)
        output = blockwise(hidden, w_down[expert])
        mixed = mixed + weight[:, None] * output.astype(jnp.float32)
        dout = (weight[:, None] * grad_out.astype(jnp.float32)).astype(jnp.bfloat16)
        dhidden = jnp.dot(dout, w_down[expert].T, preferred_element_type=jnp.float32)
        dgate = (dhidden * upper * sigma * (1.0 + gate * (1.0 - sigma))).astype(jnp.bfloat16)
        dup = (dhidden * active).astype(jnp.bfloat16)
        down_list.append(jnp.dot(hidden.T, dout, preferred_element_type=jnp.float32))
        gate_list.append(jnp.dot(tokens.T, dgate, preferred_element_type=jnp.float32))
        up_list.append(jnp.dot(tokens.T, dup, preferred_element_type=jnp.float32))
        width = dgate.shape[1] // N_TENSOR
        stacked = jnp.concatenate([w_gate[expert].T.reshape(N_TENSOR, width, -1), w_up[expert].T.reshape(N_TENSOR, width, -1)], axis=1)
        total = jnp.zeros(tokens.shape, jnp.float32)
        for block in range(N_TENSOR):
            left = jnp.concatenate([dgate[:, block * width:(block + 1) * width], dup[:, block * width:(block + 1) * width]], axis=1)
            term = jnp.dot(left, stacked[block], preferred_element_type=jnp.float32)
            term = lax.optimization_barrier(term.astype(jnp.bfloat16))
            total = total + term.astype(jnp.float32)
        dx_expert = total.astype(jnp.bfloat16)
        grad_tokens = grad_tokens + picked[:, None] * dx_expert.astype(jnp.float32)
    return (mixed.astype(jnp.bfloat16), grad_tokens.astype(jnp.bfloat16), jnp.stack(gate_list), jnp.stack(up_list), jnp.stack(down_list))
```

```python
import functools

import jax
import jax.numpy as jnp
from jax import lax
from jax.experimental import pallas as pl
from jax.experimental.pallas import tpu as pltpu
from jax.sharding import PartitionSpec as P

MESH = pl.DeviceIdType.MESH


def remote(src, dst, send_sem, recv_sem, device):
    return pltpu.make_async_remote_copy(
        src_ref=src,
        dst_ref=dst,
        send_sem=send_sem,
        recv_sem=recv_sem,
        device_id=device,
        device_id_type=MESH,
    )


def dispatch_kernel(n_dp, n_exp, n_t, send_ref, out_ref, s1, r1, s2, r2, s3, own_sem):
    d, e, t = lax.axis_index("dp"), lax.axis_index("expert"), lax.axis_index("tensor")
    width = out_ref.shape[3]
    core = lax.rem(t, 2)
    mate = t + 1 - 2 * core
    offsets = [(dd, de) for dd in range(n_dp) for de in range(n_exp)]
    offsets = offsets[1:] + offsets[:1]
    peers = [lax.rem(t + 2 * k, n_t) for k in range(1, n_t // 2)]

    def at(dp, expert, tensor):
        return (dp, expert, tensor)

    barrier = pltpu.get_barrier_semaphore()
    for dd, de in offsets[:-1]:
        pl.semaphore_signal(
            barrier,
            inc=1,
            device_id=at(lax.rem(d + dd, n_dp), lax.rem(e + de, n_exp), t),
            device_id_type=MESH,
        )
    for peer in peers + [mate]:
        pl.semaphore_signal(barrier, inc=1, device_id=at(d, e, peer), device_id_type=MESH)
    pl.semaphore_wait(barrier, len(offsets) - 1 + len(peers) + 1)

    mine = e * n_dp + d
    first = []
    for k, (dd, de) in enumerate(offsets):
        dp_to, exp_to = lax.rem(d + dd, n_dp), lax.rem(e + de, n_exp)
        block = send_ref.at[exp_to, :, pl.ds(pl.multiple_of(dp_to * width, 128), width)]
        if k == len(offsets) - 1:
            own = pltpu.make_async_copy(block, out_ref.at[t, mine], own_sem)
            own.start()
        else:
            copy = remote(block, out_ref.at[t, mine], s1.at[k], r1.at[k], at(dp_to, exp_to, t))
            copy.start()
            first.append(copy)
    second = []
    order = [len(offsets) - 1] + list(range(len(offsets) - 1))
    for k in order:
        dd, de = offsets[k]
        source = lax.rem(e + n_exp - de, n_exp) * n_dp + lax.rem(d + n_dp - dd, n_dp)
        if k == len(offsets) - 1:
            own.wait()
        else:
            remote(
                out_ref.at[t, source], out_ref.at[t, source], s1.at[k], r1.at[k], at(d, e, mate)
            ).wait_recv()
        for j, peer in enumerate(peers + [mate]):
            copy = remote(
                out_ref.at[t, source],
                out_ref.at[t, source],
                s2.at[j, k],
                r2.at[j, k],
                at(d, e, peer),
            )
            copy.start()
            second.append(copy)
    third = []
    for k in order:
        dd, de = offsets[k]
        source = lax.rem(e + n_exp - de, n_exp) * n_dp + lax.rem(d + n_dp - dd, n_dp)
        for j in range(len(peers)):
            origin = lax.rem(t + n_t - 2 * (j + 1), n_t)
            block = out_ref.at[origin, source]
            remote(block, block, s2.at[j, k], r2.at[j, k], at(d, e, mate)).wait_recv()
            copy = remote(block, block, s3.at[j, k], r2.at[len(peers) + 1 + j, k], at(d, e, mate))
            copy.start()
            third.append(copy)
    for k in order:
        dd, de = offsets[k]
        source = lax.rem(e + n_exp - de, n_exp) * n_dp + lax.rem(d + n_dp - dd, n_dp)
        block = out_ref.at[mate, source]
        remote(
            block, block, s2.at[len(peers), k], r2.at[len(peers), k], at(d, e, mate)
        ).wait_recv()
        for j in range(len(peers)):
            block = out_ref.at[lax.rem(mate + n_t - 2 * (j + 1), n_t), source]
            remote(
                block, block, s3.at[j, k], r2.at[len(peers) + 1 + j, k], at(d, e, mate)
            ).wait_recv()
    for copy in first + second + third:
        copy.wait_send()


def dispatch(send, n_dp, n_exp, n_t):
    rows, model = send.shape[1], send.shape[2]
    sources = n_dp * n_exp
    peers = n_t // 2 - 1
    return pl.pallas_call(
        functools.partial(dispatch_kernel, n_dp, n_exp, n_t),
        out_shape=jax.ShapeDtypeStruct((n_t, sources, rows, model // n_dp), jnp.bfloat16),
        in_specs=[pl.BlockSpec(memory_space=pltpu.VMEM)],
        out_specs=pl.BlockSpec(memory_space=pltpu.VMEM),
        scratch_shapes=[
            pltpu.SemaphoreType.DMA((sources,)),
            pltpu.SemaphoreType.DMA((sources,)),
            pltpu.SemaphoreType.DMA((peers + 1, sources)),
            pltpu.SemaphoreType.DMA((2 * peers + 1, sources)),
            pltpu.SemaphoreType.DMA((peers, sources)),
            pltpu.SemaphoreType.DMA,
        ],
        compiler_params=pltpu.CompilerParams(
            collective_id=0, has_side_effects=True, vmem_limit_bytes=32 * 1024 * 1024
        ),
        name="dispatch",
    )(send)


def width_sums(term_fn, total_rows):
    return lax.psum_scatter(
        term_fn(jnp.int32(0), total_rows // lax.axis_size("dp") * lax.axis_size("dp")).astype(
            jnp.bfloat16
        ),
        "dp",
        scatter_dimension=0,
        tiled=True,
    ).astype(jnp.float32)


def gather_rows(values):
    return lax.all_gather(values, "dp", axis=0, tiled=True)


def collect(partial_rows, n_exp, cap):
    n_dp = lax.axis_size("dp")
    quarter = partial_rows.shape[1]
    summed = lax.psum_scatter(
        partial_rows.astype(jnp.bfloat16), "tensor", scatter_dimension=0, tiled=True
    )
    local = summed.reshape(n_exp, n_dp * cap, quarter)
    return lax.all_to_all(
        lax.all_to_all(local, "dp", split_axis=1, concat_axis=2, tiled=True),
        "expert",
        split_axis=0,
        concat_axis=0,
        tiled=True,
    )


def body(tokens, expert_ids, gate_values, w_gate, w_up, w_down, grad_out):
    tok_rows = tokens.shape[0]
    cap = tok_rows // 2
    n_exp = lax.axis_size("expert")
    gate_mat = w_gate[0]
    up_mat = w_up[0]
    down_mat = w_down[0]
    hidden_width = gate_mat.shape[1]
    slots = jnp.arange(cap, dtype=jnp.int32)
    selector_list = []
    weight_list = []
    for expert in range(n_exp):
        chosen = (expert_ids == expert).astype(jnp.int32)
        flat_chosen = chosen.reshape(-1)
        ranks = jnp.cumsum(flat_chosen) - 1
        onehot = ((ranks[:, None] == slots[None, :]) & (flat_chosen[:, None] > 0)).astype(
            jnp.float32
        )
        selector_list.append(jnp.sum(onehot.reshape(tok_rows, 2, cap), axis=1).T)
        weight_list.append(jnp.sum(gate_values * chosen.astype(jnp.float32), axis=1))
    selector = jnp.stack(selector_list)
    weights = jnp.stack(weight_list)
    selector_bf = selector.astype(jnp.bfloat16)
    send_rows = jnp.einsum(
        "wct,td->wcd", selector_bf, tokens, preferred_element_type=jnp.float32
    ).astype(jnp.bfloat16)
    scaled = (weights[:, :, None] * grad_out.astype(jnp.float32)[None]).astype(jnp.bfloat16)
    send_grads = jnp.einsum(
        "wct,wtd->wcd", selector_bf, scaled, preferred_element_type=jnp.float32
    ).astype(jnp.bfloat16)
    n_dp, n_t = lax.axis_size("dp"), lax.axis_size("tensor")
    panels = dispatch(jnp.concatenate([send_rows, send_grads], axis=1), n_dp, n_exp, n_t)
    quarter = panels.shape[3]
    panel_rows = panels[:, :, :cap].reshape(-1, quarter)
    grad_panels = panels[:, :, cap:].reshape(-1, quarter)
    total_rows = panel_rows.shape[0]

    def forward_term(start, count):
        gate_part = jnp.dot(panel_rows, gate_mat, preferred_element_type=jnp.float32)
        up_part = jnp.dot(panel_rows, up_mat, preferred_element_type=jnp.float32)
        return jnp.concatenate([gate_part, up_part], axis=1)

    sums = width_sums(forward_term, total_rows)
    gate = sums[:, :hidden_width]
    upper = sums[:, hidden_width:]
    sigma = jax.nn.sigmoid(gate)
    active = gate * sigma
    hidden = (active * upper).astype(jnp.bfloat16)
    hidden_all = gather_rows(hidden)
    out_partial = jnp.dot(hidden_all, down_mat, preferred_element_type=jnp.float32)
    out_home = collect(out_partial, n_exp, cap)
    weighted = selector * weights[:, None, :]
    mixed = jnp.einsum(
        "wct,wcd->td", weighted, out_home.astype(jnp.float32), precision=lax.Precision.HIGHEST
    ).astype(jnp.bfloat16)
    def backward_term(start, count):
        return lax.dot_general(
            grad_panels, down_mat, (((1,), (1,)), ((), ())), preferred_element_type=jnp.float32
        )

    dhidden = width_sums(backward_term, total_rows)
    dgate = (dhidden * upper * sigma * (1.0 + gate * (1.0 - sigma))).astype(jnp.bfloat16)
    dup = (dhidden * active).astype(jnp.bfloat16)
    both_rows = jnp.concatenate([dgate, dup], axis=1)
    both_all = gather_rows(both_rows)
    dgate_all = both_all[:, :hidden_width]
    dup_all = both_all[:, hidden_width:]
    grad_down = lax.dot_general(
        hidden_all, grad_panels, (((0,), (0,)), ((), ())), preferred_element_type=jnp.float32
    )
    grad_gate = lax.dot_general(
        panel_rows, dgate_all, (((0,), (0,)), ((), ())), preferred_element_type=jnp.float32
    )
    grad_up = lax.dot_general(
        panel_rows, dup_all, (((0,), (0,)), ((), ())), preferred_element_type=jnp.float32
    )
    dx_partial = lax.dot_general(
        dgate_all, gate_mat, (((1,), (1,)), ((), ())), preferred_element_type=jnp.float32
    )
    dx_partial = dx_partial + lax.dot_general(
        dup_all, up_mat, (((1,), (1,)), ((), ())), preferred_element_type=jnp.float32
    )
    back_home = collect(dx_partial, n_exp, cap)
    grad_tokens = jnp.einsum(
        "wct,wcd->td", selector, back_home.astype(jnp.float32), precision=lax.Precision.HIGHEST
    ).astype(jnp.bfloat16)
    return (mixed, grad_tokens, grad_gate[None], grad_up[None], grad_down[None])


def solution(mesh):
    return jax.shard_map(
        body,
        mesh=mesh,
        in_specs=(
            P(("dp", "expert", "tensor"), None),
            P(("dp", "expert", "tensor"), None),
            P(("dp", "expert", "tensor"), None),
            P("expert", "dp", "tensor"),
            P("expert", "dp", "tensor"),
            P("expert", "tensor", "dp"),
            P(("dp", "expert", "tensor"), None),
        ),
        out_specs=(
            P(("dp", "expert", "tensor"), None),
            P(("dp", "expert", "tensor"), None),
            P("expert", "dp", "tensor"),
            P("expert", "dp", "tensor"),
            P("expert", "tensor", "dp"),
        ),
        check_vma=False,
    )
```

```python
import functools

import jax
import jax.numpy as jnp
from jax import lax
from jax.experimental import pallas as pl
from jax.experimental.pallas import tpu as pltpu
from jax.sharding import PartitionSpec as P

MESH = pl.DeviceIdType.MESH


def remote(src, dst, send_sem, recv_sem, device):
    return pltpu.make_async_remote_copy(
        src_ref=src,
        dst_ref=dst,
        send_sem=send_sem,
        recv_sem=recv_sem,
        device_id=device,
        device_id_type=MESH,
    )


def dispatch_kernel(n_dp, n_exp, n_t, send_ref, out_ref, s1, r1, s2, r2, s3, own_sem):
    d, e, t = lax.axis_index("dp"), lax.axis_index("expert"), lax.axis_index("tensor")
    width = out_ref.shape[3]
    core = lax.rem(t, 2)
    mate = t + 1 - 2 * core
    offsets = [(dd, de) for dd in range(n_dp) for de in range(n_exp)]
    offsets = offsets[1:] + offsets[:1]
    peers = [lax.rem(t + 2 * k, n_t) for k in range(1, n_t // 2)]

    def at(dp, expert, tensor):
        return (dp, expert, tensor)

    barrier = pltpu.get_barrier_semaphore()
    for dd, de in offsets[:-1]:
        pl.semaphore_signal(
            barrier,
            inc=1,
            device_id=at(lax.rem(d + dd, n_dp), lax.rem(e + de, n_exp), t),
            device_id_type=MESH,
        )
    for peer in peers + [mate]:
        pl.semaphore_signal(barrier, inc=1, device_id=at(d, e, peer), device_id_type=MESH)
    pl.semaphore_wait(barrier, len(offsets) - 1 + len(peers) + 1)

    mine = e * n_dp + d
    first = []
    for k, (dd, de) in enumerate(offsets):
        dp_to, exp_to = lax.rem(d + dd, n_dp), lax.rem(e + de, n_exp)
        block = send_ref.at[exp_to, :, pl.ds(pl.multiple_of(dp_to * width, 128), width)]
        if k == len(offsets) - 1:
            own = pltpu.make_async_copy(block, out_ref.at[t, mine], own_sem)
            own.start()
        else:
            copy = remote(block, out_ref.at[t, mine], s1.at[k], r1.at[k], at(dp_to, exp_to, t))
            copy.start()
            first.append(copy)
    second = []
    order = [len(offsets) - 1] + list(range(len(offsets) - 1))
    for k in order:
        dd, de = offsets[k]
        source = lax.rem(e + n_exp - de, n_exp) * n_dp + lax.rem(d + n_dp - dd, n_dp)
        if k == len(offsets) - 1:
            own.wait()
        else:
            remote(
                out_ref.at[t, source], out_ref.at[t, source], s1.at[k], r1.at[k], at(d, e, mate)
            ).wait_recv()
        for j, peer in enumerate(peers + [mate]):
            copy = remote(
                out_ref.at[t, source],
                out_ref.at[t, source],
                s2.at[j, k],
                r2.at[j, k],
                at(d, e, peer),
            )
            copy.start()
            second.append(copy)
    third = []
    for k in order:
        dd, de = offsets[k]
        source = lax.rem(e + n_exp - de, n_exp) * n_dp + lax.rem(d + n_dp - dd, n_dp)
        for j in range(len(peers)):
            origin = lax.rem(t + n_t - 2 * (j + 1), n_t)
            block = out_ref.at[origin, source]
            remote(block, block, s2.at[j, k], r2.at[j, k], at(d, e, mate)).wait_recv()
            copy = remote(block, block, s3.at[j, k], r2.at[len(peers) + 1 + j, k], at(d, e, mate))
            copy.start()
            third.append(copy)
    for k in order:
        dd, de = offsets[k]
        source = lax.rem(e + n_exp - de, n_exp) * n_dp + lax.rem(d + n_dp - dd, n_dp)
        block = out_ref.at[mate, source]
        remote(
            block, block, s2.at[len(peers), k], r2.at[len(peers), k], at(d, e, mate)
        ).wait_recv()
        for j in range(len(peers)):
            block = out_ref.at[lax.rem(mate + n_t - 2 * (j + 1), n_t), source]
            remote(
                block, block, s3.at[j, k], r2.at[len(peers) + 1 + j, k], at(d, e, mate)
            ).wait_recv()
    for copy in first + second + third:
        copy.wait_send()


def dispatch(send, n_dp, n_exp, n_t):
    rows, model = send.shape[1], send.shape[2]
    sources = n_dp * n_exp
    peers = n_t // 2 - 1
    return pl.pallas_call(
        functools.partial(dispatch_kernel, n_dp, n_exp, n_t),
        out_shape=jax.ShapeDtypeStruct((n_t, sources, rows, model // n_dp), jnp.bfloat16),
        in_specs=[pl.BlockSpec(memory_space=pltpu.VMEM)],
        out_specs=pl.BlockSpec(memory_space=pltpu.VMEM),
        scratch_shapes=[
            pltpu.SemaphoreType.DMA((sources,)),
            pltpu.SemaphoreType.DMA((sources,)),
            pltpu.SemaphoreType.DMA((peers + 1, sources)),
            pltpu.SemaphoreType.DMA((2 * peers + 1, sources)),
            pltpu.SemaphoreType.DMA((peers, sources)),
            pltpu.SemaphoreType.DMA,
        ],
        compiler_params=pltpu.CompilerParams(
            collective_id=0, has_side_effects=True, vmem_limit_bytes=32 * 1024 * 1024
        ),
        name="dispatch",
    )(send)


LAG = 2


def chain_kernel(
    n, x_ref, g_ref, wg_ref, wu_ref, wd_ref, act_ref, vg, vu, vd, rbuf, sbuf, acc, wsem, rs_s, rs_r, ag_s, ag_r
):
    d, e, t = lax.axis_index("dp"), lax.axis_index("expert"), lax.axis_index("tensor")
    n_chunks, hc = vd.shape[0], vd.shape[1]
    half = x_ref.shape[0] // 2

    @pl.when(d > 0)
    def _():
        pl.semaphore_signal(
            pltpu.get_barrier_semaphore(), inc=1, device_id=(d - 1, e, t), device_id_type=MESH
        )

    @pl.when(d < n - 1)
    def _():
        pl.semaphore_signal(
            pltpu.get_barrier_semaphore(), inc=1, device_id=(d + 1, e, t), device_id_type=MESH
        )

    def loads(c):
        cols = pl.ds(pl.multiple_of(c * hc, 128), hc)
        return (
            pltpu.make_async_copy(wg_ref.at[:, cols], vg.at[c], wsem.at[0, c]),
            pltpu.make_async_copy(wu_ref.at[:, cols], vu.at[c], wsem.at[1, c]),
            pltpu.make_async_copy(wd_ref.at[cols, :], vd.at[c], wsem.at[2, c]),
        )

    @pl.loop(0, n_chunks)
    def _(c):
        for copy in loads(c):
            copy.start()

    @pl.when((d > 0) & (d < n - 1))
    def _():
        pl.semaphore_wait(pltpu.get_barrier_semaphore(), 2)

    @pl.when((d == 0) | (d == n - 1))
    def _():
        pl.semaphore_wait(pltpu.get_barrier_semaphore(), 1)

    def chain(s):
        return (d, d - 1, d + 1) if s == 0 else (n - 1 - d, d + 1, d - 1)

    def window(s, c):
        return act_ref.at[:, pl.ds(s * half, half), pl.ds(pl.multiple_of(c * hc, 128), hc)]

    def up_copy(s, c):
        up = chain(s)[1]
        return remote(sbuf.at[s, c], rbuf.at[s, c], rs_s.at[s, c], rs_r.at[s, c], (up, e, t))

    def down_copy(s, c):
        down = chain(s)[2]
        return remote(window(s, c), window(s, c), ag_s.at[s, c], ag_r.at[s, c], (down, e, t))

    def spread_step(s, i):
        p = chain(s)[0]
        c = i - LAG * (n - 1) - LAG * p

        @pl.when((p > 0) & (c >= 0) & (c < n_chunks))
        def _():
            down_copy(s, c).wait_recv()

            @pl.when(p < n - 1)
            def _():
                down_copy(s, c).start()

    def sum_step(s, i):
        p = chain(s)[0]
        c = i - LAG * (n - 1 - p)

        @pl.when((c >= 0) & (c < n_chunks))
        def _():
            x = x_ref[pl.ds(s * half, half), :]
            g = g_ref[pl.ds(s * half, half), :]
            acc[0] = jnp.dot(x, vg[c], preferred_element_type=jnp.float32)
            acc[1] = jnp.dot(x, vu[c], preferred_element_type=jnp.float32)
            acc[2] = lax.dot_general(
                g, vd[c], (((1,), (1,)), ((), ())), preferred_element_type=jnp.float32
            )

            @pl.when(p < n - 1)
            def _():
                up_copy(s, c).wait_recv()
                acc[...] += rbuf[s, c].astype(jnp.float32)

            @pl.when(p > 0)
            def _():
                sbuf[s, c] = acc[...].astype(jnp.bfloat16)
                up_copy(s, c).start()

            @pl.when(p == 0)
            def _():
                gate, upper, dhidden = acc[0], acc[1], acc[2]
                sigma = jax.nn.sigmoid(gate)
                active = gate * sigma
                rows = pl.ds(s * half, half)
                cols = pl.ds(pl.multiple_of(c * hc, 128), hc)
                act_ref[0, rows, cols] = (active * upper).astype(jnp.bfloat16)
                act_ref[1, rows, cols] = (
                    dhidden * upper * sigma * (1.0 + gate * (1.0 - sigma))
                ).astype(jnp.bfloat16)
                act_ref[2, rows, cols] = (dhidden * active).astype(jnp.bfloat16)
                down_copy(s, c).start()

    @pl.loop(0, n_chunks + 2 * LAG * (n - 1))
    def _(i):
        @pl.when(i < n_chunks)
        def _():
            for copy in loads(i):
                copy.wait()

        for s in range(2):
            spread_step(s, i)
        for s in range(2):
            sum_step(s, i)

    @pl.loop(0, n_chunks)
    def _(c):
        for s in range(2):
            p = chain(s)[0]

            @pl.when(p > 0)
            def _():
                up_copy(s, c).wait_send()

            @pl.when(p < n - 1)
            def _():
                down_copy(s, c).wait_send()


def hidden_grads(x, g, wg, wu, wd, n_dp):
    rows, quarter = x.shape
    hidden = wg.shape[1]
    hc = 128
    nc = hidden // hc
    vmem = pl.BlockSpec(memory_space=pltpu.VMEM)
    anywhere = pl.BlockSpec(memory_space=pl.ANY)
    return pl.pallas_call(
        functools.partial(chain_kernel, n_dp),
        out_shape=jax.ShapeDtypeStruct((3, rows, hidden), jnp.bfloat16),
        in_specs=[vmem, vmem, anywhere, anywhere, anywhere],
        out_specs=vmem,
        scratch_shapes=[
            pltpu.VMEM((nc, quarter, hc), jnp.bfloat16),
            pltpu.VMEM((nc, quarter, hc), jnp.bfloat16),
            pltpu.VMEM((nc, hc, quarter), jnp.bfloat16),
            pltpu.VMEM((2, nc, 3, rows // 2, hc), jnp.bfloat16),
            pltpu.VMEM((2, nc, 3, rows // 2, hc), jnp.bfloat16),
            pltpu.VMEM((3, rows // 2, hc), jnp.float32),
            pltpu.SemaphoreType.DMA((3, nc)),
            pltpu.SemaphoreType.DMA((2, nc)),
            pltpu.SemaphoreType.DMA((2, nc)),
            pltpu.SemaphoreType.DMA((2, nc)),
            pltpu.SemaphoreType.DMA((2, nc)),
        ],
        compiler_params=pltpu.CompilerParams(
            collective_id=1, has_side_effects=True, vmem_limit_bytes=44 * 1024 * 1024
        ),
        name="chain",
    )(x, g, wg, wu, wd)


def collect(partial_rows, n_exp, cap):
    n_dp = lax.axis_size("dp")
    quarter = partial_rows.shape[1]
    summed = lax.psum_scatter(
        partial_rows.astype(jnp.bfloat16), "tensor", scatter_dimension=0, tiled=True
    )
    local = summed.reshape(n_exp, n_dp * cap, quarter)
    return lax.all_to_all(
        lax.all_to_all(local, "dp", split_axis=1, concat_axis=2, tiled=True),
        "expert",
        split_axis=0,
        concat_axis=0,
        tiled=True,
    )


def body(tokens, expert_ids, gate_values, w_gate, w_up, w_down, grad_out):
    tok_rows = tokens.shape[0]
    cap = tok_rows // 2
    n_exp = lax.axis_size("expert")
    gate_mat = w_gate[0]
    up_mat = w_up[0]
    down_mat = w_down[0]
    slots = jnp.arange(cap, dtype=jnp.int32)
    selector_list = []
    weight_list = []
    for expert in range(n_exp):
        chosen = (expert_ids == expert).astype(jnp.int32)
        flat_chosen = chosen.reshape(-1)
        ranks = jnp.cumsum(flat_chosen) - 1
        onehot = ((ranks[:, None] == slots[None, :]) & (flat_chosen[:, None] > 0)).astype(
            jnp.float32
        )
        selector_list.append(jnp.sum(onehot.reshape(tok_rows, 2, cap), axis=1).T)
        weight_list.append(jnp.sum(gate_values * chosen.astype(jnp.float32), axis=1))
    selector = jnp.stack(selector_list)
    weights = jnp.stack(weight_list)
    selector_bf = selector.astype(jnp.bfloat16)
    send_rows = jnp.einsum(
        "wct,td->wcd", selector_bf, tokens, preferred_element_type=jnp.float32
    ).astype(jnp.bfloat16)
    scaled = (weights[:, :, None] * grad_out.astype(jnp.float32)[None]).astype(jnp.bfloat16)
    send_grads = jnp.einsum(
        "wct,wtd->wcd", selector_bf, scaled, preferred_element_type=jnp.float32
    ).astype(jnp.bfloat16)
    n_dp, n_t = lax.axis_size("dp"), lax.axis_size("tensor")
    panels = dispatch(jnp.concatenate([send_rows, send_grads], axis=1), n_dp, n_exp, n_t)
    quarter = panels.shape[3]
    panel_rows = panels[:, :, :cap].reshape(-1, quarter)
    grad_panels = panels[:, :, cap:].reshape(-1, quarter)

    hidden_all, dgate_all, dup_all = hidden_grads(
        panel_rows, grad_panels, gate_mat, up_mat, down_mat, n_dp
    )
    out_partial = jnp.dot(hidden_all, down_mat, preferred_element_type=jnp.float32)
    out_home = collect(out_partial, n_exp, cap)
    weighted = selector * weights[:, None, :]
    mixed = jnp.einsum(
        "wct,wcd->td", weighted, out_home.astype(jnp.float32), precision=lax.Precision.HIGHEST
    ).astype(jnp.bfloat16)
    grad_down = lax.dot_general(
        hidden_all, grad_panels, (((0,), (0,)), ((), ())), preferred_element_type=jnp.float32
    )
    grad_gate = lax.dot_general(
        panel_rows, dgate_all, (((0,), (0,)), ((), ())), preferred_element_type=jnp.float32
    )
    grad_up = lax.dot_general(
        panel_rows, dup_all, (((0,), (0,)), ((), ())), preferred_element_type=jnp.float32
    )
    dx_partial = lax.dot_general(
        dgate_all, gate_mat, (((1,), (1,)), ((), ())), preferred_element_type=jnp.float32
    )
    dx_partial = dx_partial + lax.dot_general(
        dup_all, up_mat, (((1,), (1,)), ((), ())), preferred_element_type=jnp.float32
    )
    back_home = collect(dx_partial, n_exp, cap)
    grad_tokens = jnp.einsum(
        "wct,wcd->td", selector, back_home.astype(jnp.float32), precision=lax.Precision.HIGHEST
    ).astype(jnp.bfloat16)
    return (mixed, grad_tokens, grad_gate[None], grad_up[None], grad_down[None])


def solution(mesh):
    return jax.shard_map(
        body,
        mesh=mesh,
        in_specs=(
            P(("dp", "expert", "tensor"), None),
            P(("dp", "expert", "tensor"), None),
            P(("dp", "expert", "tensor"), None),
            P("expert", "dp", "tensor"),
            P("expert", "dp", "tensor"),
            P("expert", "tensor", "dp"),
            P(("dp", "expert", "tensor"), None),
        ),
        out_specs=(
            P(("dp", "expert", "tensor"), None),
            P(("dp", "expert", "tensor"), None),
            P("expert", "dp", "tensor"),
            P("expert", "dp", "tensor"),
            P("expert", "tensor", "dp"),
        ),
        check_vma=False,
    )
```

```python
import functools

import jax
import jax.numpy as jnp
from jax import lax
from jax.experimental import pallas as pl
from jax.experimental.pallas import tpu as pltpu
from jax.sharding import PartitionSpec as P

MESH = pl.DeviceIdType.MESH


def remote(src, dst, send_sem, recv_sem, device):
    return pltpu.make_async_remote_copy(
        src_ref=src,
        dst_ref=dst,
        send_sem=send_sem,
        recv_sem=recv_sem,
        device_id=device,
        device_id_type=MESH,
    )


def dispatch_kernel(n_dp, n_exp, n_t, send_ref, out_ref, s1, r1, s2, r2, s3, own_sem):
    d, e, t = lax.axis_index("dp"), lax.axis_index("expert"), lax.axis_index("tensor")
    width = out_ref.shape[3]
    core = lax.rem(t, 2)
    mate = t + 1 - 2 * core
    offsets = [(dd, de) for dd in range(n_dp) for de in range(n_exp)]
    offsets = offsets[1:] + offsets[:1]
    peers = [lax.rem(t + 2 * k, n_t) for k in range(1, n_t // 2)]

    def at(dp, expert, tensor):
        return (dp, expert, tensor)

    barrier = pltpu.get_barrier_semaphore()
    for dd, de in offsets[:-1]:
        pl.semaphore_signal(
            barrier,
            inc=1,
            device_id=at(lax.rem(d + dd, n_dp), lax.rem(e + de, n_exp), t),
            device_id_type=MESH,
        )
    for peer in peers + [mate]:
        pl.semaphore_signal(barrier, inc=1, device_id=at(d, e, peer), device_id_type=MESH)
    pl.semaphore_wait(barrier, len(offsets) - 1 + len(peers) + 1)

    mine = e * n_dp + d
    first = []
    for k, (dd, de) in enumerate(offsets):
        dp_to, exp_to = lax.rem(d + dd, n_dp), lax.rem(e + de, n_exp)
        block = send_ref.at[exp_to, :, pl.ds(pl.multiple_of(dp_to * width, 128), width)]
        if k == len(offsets) - 1:
            own = pltpu.make_async_copy(block, out_ref.at[t, mine], own_sem)
            own.start()
        else:
            copy = remote(block, out_ref.at[t, mine], s1.at[k], r1.at[k], at(dp_to, exp_to, t))
            copy.start()
            first.append(copy)
    second = []
    order = [len(offsets) - 1] + list(range(len(offsets) - 1))
    for k in order:
        dd, de = offsets[k]
        source = lax.rem(e + n_exp - de, n_exp) * n_dp + lax.rem(d + n_dp - dd, n_dp)
        if k == len(offsets) - 1:
            own.wait()
        else:
            remote(
                out_ref.at[t, source], out_ref.at[t, source], s1.at[k], r1.at[k], at(d, e, mate)
            ).wait_recv()
        for j, peer in enumerate(peers + [mate]):
            copy = remote(
                out_ref.at[t, source],
                out_ref.at[t, source],
                s2.at[j, k],
                r2.at[j, k],
                at(d, e, peer),
            )
            copy.start()
            second.append(copy)
    third = []
    for k in order:
        dd, de = offsets[k]
        source = lax.rem(e + n_exp - de, n_exp) * n_dp + lax.rem(d + n_dp - dd, n_dp)
        for j in range(len(peers)):
            origin = lax.rem(t + n_t - 2 * (j + 1), n_t)
            block = out_ref.at[origin, source]
            remote(block, block, s2.at[j, k], r2.at[j, k], at(d, e, mate)).wait_recv()
            copy = remote(block, block, s3.at[j, k], r2.at[len(peers) + 1 + j, k], at(d, e, mate))
            copy.start()
            third.append(copy)
    for k in order:
        dd, de = offsets[k]
        source = lax.rem(e + n_exp - de, n_exp) * n_dp + lax.rem(d + n_dp - dd, n_dp)
        block = out_ref.at[mate, source]
        remote(
            block, block, s2.at[len(peers), k], r2.at[len(peers), k], at(d, e, mate)
        ).wait_recv()
        for j in range(len(peers)):
            block = out_ref.at[lax.rem(mate + n_t - 2 * (j + 1), n_t), source]
            remote(
                block, block, s3.at[j, k], r2.at[len(peers) + 1 + j, k], at(d, e, mate)
            ).wait_recv()
    for copy in first + second + third:
        copy.wait_send()


def dispatch(send, n_dp, n_exp, n_t):
    rows, model = send.shape[1], send.shape[2]
    sources = n_dp * n_exp
    peers = n_t // 2 - 1
    return pl.pallas_call(
        functools.partial(dispatch_kernel, n_dp, n_exp, n_t),
        out_shape=jax.ShapeDtypeStruct((n_t, sources, rows, model // n_dp), jnp.bfloat16),
        in_specs=[pl.BlockSpec(memory_space=pltpu.VMEM)],
        out_specs=pl.BlockSpec(memory_space=pltpu.VMEM),
        scratch_shapes=[
            pltpu.SemaphoreType.DMA((sources,)),
            pltpu.SemaphoreType.DMA((sources,)),
            pltpu.SemaphoreType.DMA((peers + 1, sources)),
            pltpu.SemaphoreType.DMA((2 * peers + 1, sources)),
            pltpu.SemaphoreType.DMA((peers, sources)),
            pltpu.SemaphoreType.DMA,
        ],
        compiler_params=pltpu.CompilerParams(
            collective_id=0, has_side_effects=True, vmem_limit_bytes=32 * 1024 * 1024
        ),
        name="dispatch",
    )(send)


LAG = 2


def chain_kernel(
    n, x_ref, g_ref, wg_ref, wu_ref, wd_ref, act_ref, part_ref,
    vgu, vd, part, rbuf, sbuf, out_acc, dx_acc, wsem, rs_s, rs_r, ag_s, ag_r
):
    d, e, t = lax.axis_index("dp"), lax.axis_index("expert"), lax.axis_index("tensor")
    n_chunks, hc = vd.shape[0], vd.shape[1]
    half = x_ref.shape[0] // 2

    @pl.when(d > 0)
    def _():
        pl.semaphore_signal(
            pltpu.get_barrier_semaphore(), inc=1, device_id=(d - 1, e, t), device_id_type=MESH
        )

    @pl.when(d < n - 1)
    def _():
        pl.semaphore_signal(
            pltpu.get_barrier_semaphore(), inc=1, device_id=(d + 1, e, t), device_id_type=MESH
        )

    def loads(c):
        cols = pl.ds(pl.multiple_of(c * hc, 128), hc)
        return (
            pltpu.make_async_copy(wg_ref.at[:, cols], vgu.at[c, :, pl.ds(0, hc)], wsem.at[0, c]),
            pltpu.make_async_copy(wu_ref.at[:, cols], vgu.at[c, :, pl.ds(hc, hc)], wsem.at[1, c]),
            pltpu.make_async_copy(wd_ref.at[cols, :], vd.at[c], wsem.at[2, c]),
        )

    @pl.loop(0, n_chunks)
    def _(c):
        for copy in loads(c):
            copy.start()

    @pl.when((d > 0) & (d < n - 1))
    def _():
        pl.semaphore_wait(pltpu.get_barrier_semaphore(), 2)

    @pl.when((d == 0) | (d == n - 1))
    def _():
        pl.semaphore_wait(pltpu.get_barrier_semaphore(), 1)

    def chain(s):
        return (d, d - 1, d + 1) if s == 0 else (n - 1 - d, d + 1, d - 1)

    def window(s, c):
        return act_ref.at[:, pl.ds(s * half, half), pl.ds(pl.multiple_of(c * hc, 128), hc)]

    def up_copy(s, c):
        up = chain(s)[1]
        return remote(sbuf.at[s, c], rbuf.at[s, c], rs_s.at[s, c], rs_r.at[s, c], (up, e, t))

    def down_copy(s, c):
        down = chain(s)[2]
        return remote(window(s, c), window(s, c), ag_s.at[s, c], ag_r.at[s, c], (down, e, t))

    def spread_step(s, i):
        p = chain(s)[0]
        c = i - LAG * (n - 1) - LAG * p

        @pl.when((p > 0) & (c >= 0) & (c < n_chunks))
        def _():
            down_copy(s, c).wait_recv()

            @pl.when(p < n - 1)
            def _():
                down_copy(s, c).start()

    def sum_step(s, i):
        p = chain(s)[0]
        c = i - LAG * (n - 1 - p)

        @pl.when((c >= 0) & (c < n_chunks))
        def _():
            rows = pl.ds(s * half, half)

            @pl.when(p < n - 1)
            def _():
                up_copy(s, c).wait_recv()
                part[c, rows, :] += rbuf[s, c].astype(jnp.float32)

            @pl.when(p > 0)
            def _():
                sbuf[s, c] = part[c, rows, :].astype(jnp.bfloat16)
                up_copy(s, c).start()

            @pl.when(p == 0)
            def _():
                gate = part[c, rows, pl.ds(0, hc)]
                upper = part[c, rows, pl.ds(hc, hc)]
                dhidden = part[c, rows, pl.ds(2 * hc, hc)]
                sigma = jax.nn.sigmoid(gate)
                active = gate * sigma
                cols = pl.ds(pl.multiple_of(c * hc, 128), hc)
                act_ref[0, rows, cols] = (active * upper).astype(jnp.bfloat16)
                act_ref[1, rows, cols] = (
                    dhidden * upper * sigma * (1.0 + gate * (1.0 - sigma))
                ).astype(jnp.bfloat16)
                act_ref[2, rows, cols] = (dhidden * active).astype(jnp.bfloat16)
                down_copy(s, c).start()

    def output_step(c):
        cols = pl.ds(pl.multiple_of(c * hc, 128), hc)
        out_acc[...] += jnp.dot(
            act_ref[0, :, cols], vd[c], preferred_element_type=jnp.float32
        )
        both = jnp.concatenate([act_ref[1, :, cols], act_ref[2, :, cols]], axis=1)
        dx_acc[...] += lax.dot_general(
            both, vgu[c], (((1,), (1,)), ((), ())), preferred_element_type=jnp.float32
        )

    out_acc[...] = jnp.zeros_like(out_acc)
    dx_acc[...] = jnp.zeros_like(dx_acc)

    @pl.loop(0, n_chunks + 2 * LAG * (n - 1))
    def _(i):
        @pl.when(i < n_chunks)
        def _():
            for copy in loads(i):
                copy.wait()
            part[i, :, pl.ds(0, 2 * hc)] = jnp.dot(
                x_ref[...], vgu[i], preferred_element_type=jnp.float32
            )
            part[i, :, pl.ds(2 * hc, hc)] = lax.dot_general(
                g_ref[...], vd[i], (((1,), (1,)), ((), ())), preferred_element_type=jnp.float32
            )

        for s in range(2):
            spread_step(s, i)
        for s in range(2):
            sum_step(s, i)

        @pl.when(i >= 2 * LAG * (n - 1))
        def _():
            output_step(i - 2 * LAG * (n - 1))

    cap = part_ref.shape[1] // 2

    @pl.loop(0, part_ref.shape[0])
    def _(b):
        rows = pl.ds(pl.multiple_of(b * cap, 8), cap)
        part_ref[b] = jnp.concatenate([out_acc[rows, :], dx_acc[rows, :]], axis=0).astype(
            jnp.bfloat16
        )

    @pl.loop(0, n_chunks)
    def _(c):
        for s in range(2):
            p = chain(s)[0]

            @pl.when(p > 0)
            def _():
                up_copy(s, c).wait_send()

            @pl.when(p < n - 1)
            def _():
                down_copy(s, c).wait_send()


def hidden_grads(x, g, wg, wu, wd, n_dp, cap):
    rows, quarter = x.shape
    hidden = wg.shape[1]
    hc = 128
    nc = hidden // hc
    vmem = pl.BlockSpec(memory_space=pltpu.VMEM)
    anywhere = pl.BlockSpec(memory_space=pl.ANY)
    return pl.pallas_call(
        functools.partial(chain_kernel, n_dp),
        out_shape=(
            jax.ShapeDtypeStruct((3, rows, hidden), jnp.bfloat16),
            jax.ShapeDtypeStruct((rows // cap, 2 * cap, quarter), jnp.bfloat16),
        ),
        in_specs=[vmem, vmem, anywhere, anywhere, anywhere],
        out_specs=(vmem, vmem),
        scratch_shapes=[
            pltpu.VMEM((nc, quarter, 2 * hc), jnp.bfloat16),
            pltpu.VMEM((nc, hc, quarter), jnp.bfloat16),
            pltpu.VMEM((nc, rows, 3 * hc), jnp.float32),
            pltpu.VMEM((2, nc, rows // 2, 3 * hc), jnp.bfloat16),
            pltpu.VMEM((2, nc, rows // 2, 3 * hc), jnp.bfloat16),
            pltpu.VMEM((rows, quarter), jnp.float32),
            pltpu.VMEM((rows, quarter), jnp.float32),
            pltpu.SemaphoreType.DMA((3, nc)),
            pltpu.SemaphoreType.DMA((2, nc)),
            pltpu.SemaphoreType.DMA((2, nc)),
            pltpu.SemaphoreType.DMA((2, nc)),
            pltpu.SemaphoreType.DMA((2, nc)),
        ],
        compiler_params=pltpu.CompilerParams(
            collective_id=1, has_side_effects=True, vmem_limit_bytes=54 * 1024 * 1024
        ),
        name="chain",
    )(x, g, wg, wu, wd)


def collect_kernel(
    n_dp, n_exp, n_t, part_ref, home_ref, in_a, pair, in_b, total, a_s, a_r, b_s, b_r, c_s, c_r
):
    d, e, t = lax.axis_index("dp"), lax.axis_index("expert"), lax.axis_index("tensor")
    width = part_ref.shape[3]
    core = lax.rem(t, 2)
    mate = t + 1 - 2 * core
    n_hi = n_t // 2
    offsets = [(dd, de) for dd in range(n_dp) for de in range(n_exp)]
    offsets = offsets[1:] + offsets[:1]
    last = len(offsets) - 1

    def source(k):
        dd, de = offsets[k]
        return lax.rem(e + de, n_exp) * n_dp + lax.rem(d + dd, n_dp)

    barrier = pltpu.get_barrier_semaphore()
    for dd, de in offsets[:-1]:
        pl.semaphore_signal(
            barrier,
            inc=1,
            device_id=(lax.rem(d + dd, n_dp), lax.rem(e + de, n_exp), t),
            device_id_type=MESH,
        )
    for peer in [lax.rem(t + 2 * j, n_t) for j in range(1, n_hi)] + [mate]:
        pl.semaphore_signal(barrier, inc=1, device_id=(d, e, peer), device_id_type=MESH)
    pl.semaphore_wait(barrier, last + n_hi)

    order = list(range(1, n_hi)) + [0]
    swaps = {}
    for j in order:
        swaps[j] = remote(
            part_ref.at[lax.rem(mate + 2 * j, n_t)],
            in_a.at[j],
            a_s.at[j],
            a_r.at[j],
            (d, e, mate),
        )
        swaps[j].start()
    sums = []
    for j in order[:-1]:
        swaps[j].wait_recv()
        peer = lax.rem(t + 2 * j, n_t)
        for k in range(last + 1):
            where = source(k)
            pair[j - 1, k] = (
                part_ref[peer, where].astype(jnp.float32) + in_a[j, where].astype(jnp.float32)
            ).astype(jnp.bfloat16)
            copy = remote(
                pair.at[j - 1, k],
                in_b.at[j - 1, k],
                b_s.at[j - 1, k],
                b_r.at[j - 1, k],
                (d, e, peer),
            )
            copy.start()
            sums.append(copy)
    swaps[0].wait_recv()
    homes = []
    for k in range(last + 1):
        where = source(k)
        value = part_ref[t, where].astype(jnp.float32) + in_a[0, where].astype(jnp.float32)
        for j in order[:-1]:
            sums[(j - 1) * (last + 1) + k].wait_recv()
            value = value + in_b[j - 1, k].astype(jnp.float32)
        columns = pl.ds(pl.multiple_of(d * width, 128), width)
        if k == last:
            home_ref[e, :, columns] = value.astype(jnp.bfloat16)
        else:
            total[k] = value.astype(jnp.bfloat16)
            dd, de = offsets[k]
            copy = remote(
                total.at[k],
                home_ref.at[e, :, columns],
                c_s.at[k],
                c_r.at[k],
                (lax.rem(d + dd, n_dp), lax.rem(e + de, n_exp), t),
            )
            copy.start()
            homes.append(copy)
    for k in range(last):
        dd, de = offsets[k]
        from_dp, from_exp = lax.rem(d + n_dp - dd, n_dp), lax.rem(e + n_exp - de, n_exp)
        columns = pl.ds(pl.multiple_of(from_dp * width, 128), width)
        remote(
            total.at[k], home_ref.at[from_exp, :, columns], c_s.at[k], c_r.at[k], (d, e, mate)
        ).wait_recv()
    for copy in list(swaps.values()) + sums + homes:
        copy.wait_send()


def collect(part, n_dp, n_exp, n_t):
    rows, width = part.shape[2], part.shape[3]
    sources, n_hi = n_dp * n_exp, n_t // 2
    vmem = pl.BlockSpec(memory_space=pltpu.VMEM)
    return pl.pallas_call(
        functools.partial(collect_kernel, n_dp, n_exp, n_t),
        out_shape=jax.ShapeDtypeStruct((n_exp, rows, n_dp * width), jnp.bfloat16),
        in_specs=[vmem],
        out_specs=vmem,
        scratch_shapes=[
            pltpu.VMEM((n_hi, sources, rows, width), jnp.bfloat16),
            pltpu.VMEM((n_hi - 1, sources, rows, width), jnp.bfloat16),
            pltpu.VMEM((n_hi - 1, sources, rows, width), jnp.bfloat16),
            pltpu.VMEM((sources - 1, rows, width), jnp.bfloat16),
            pltpu.SemaphoreType.DMA((n_hi,)),
            pltpu.SemaphoreType.DMA((n_hi,)),
            pltpu.SemaphoreType.DMA((n_hi - 1, sources)),
            pltpu.SemaphoreType.DMA((n_hi - 1, sources)),
            pltpu.SemaphoreType.DMA((sources - 1,)),
            pltpu.SemaphoreType.DMA((sources - 1,)),
        ],
        compiler_params=pltpu.CompilerParams(
            collective_id=2, has_side_effects=True, vmem_limit_bytes=32 * 1024 * 1024
        ),
        name="collect",
    )(part)


def body(tokens, expert_ids, gate_values, w_gate, w_up, w_down, grad_out):
    tok_rows = tokens.shape[0]
    cap = tok_rows // 2
    n_exp = lax.axis_size("expert")
    gate_mat = w_gate[0]
    up_mat = w_up[0]
    down_mat = w_down[0]
    slots = jnp.arange(cap, dtype=jnp.int32)
    selector_list = []
    weight_list = []
    for expert in range(n_exp):
        chosen = (expert_ids == expert).astype(jnp.int32)
        flat_chosen = chosen.reshape(-1)
        ranks = jnp.cumsum(flat_chosen) - 1
        onehot = ((ranks[:, None] == slots[None, :]) & (flat_chosen[:, None] > 0)).astype(
            jnp.float32
        )
        selector_list.append(jnp.sum(onehot.reshape(tok_rows, 2, cap), axis=1).T)
        weight_list.append(jnp.sum(gate_values * chosen.astype(jnp.float32), axis=1))
    selector = jnp.stack(selector_list)
    weights = jnp.stack(weight_list)
    selector_bf = selector.astype(jnp.bfloat16)
    send_rows = jnp.einsum(
        "wct,td->wcd", selector_bf, tokens, preferred_element_type=jnp.float32
    ).astype(jnp.bfloat16)
    scaled = (weights[:, :, None] * grad_out.astype(jnp.float32)[None]).astype(jnp.bfloat16)
    send_grads = jnp.einsum(
        "wct,wtd->wcd", selector_bf, scaled, preferred_element_type=jnp.float32
    ).astype(jnp.bfloat16)
    n_dp, n_t = lax.axis_size("dp"), lax.axis_size("tensor")
    panels = dispatch(jnp.concatenate([send_rows, send_grads], axis=1), n_dp, n_exp, n_t)
    quarter = panels.shape[3]
    panel_rows = panels[:, :, :cap].reshape(-1, quarter)
    grad_panels = panels[:, :, cap:].reshape(-1, quarter)

    acts, part = hidden_grads(panel_rows, grad_panels, gate_mat, up_mat, down_mat, n_dp, cap)
    hidden_all, dgate_all, dup_all = acts
    home = collect(part.reshape(panels.shape), n_dp, n_exp, n_t)
    out_home, back_home = home[:, :cap], home[:, cap:]
    weighted = selector * weights[:, None, :]
    mixed = jnp.einsum(
        "wct,wcd->td", weighted, out_home.astype(jnp.float32), precision=lax.Precision.HIGHEST
    ).astype(jnp.bfloat16)
    grad_down = lax.dot_general(
        hidden_all, grad_panels, (((0,), (0,)), ((), ())), preferred_element_type=jnp.float32
    )
    grad_gate = lax.dot_general(
        panel_rows, dgate_all, (((0,), (0,)), ((), ())), preferred_element_type=jnp.float32
    )
    grad_up = lax.dot_general(
        panel_rows, dup_all, (((0,), (0,)), ((), ())), preferred_element_type=jnp.float32
    )
    grad_tokens = jnp.einsum(
        "wct,wcd->td", selector, back_home.astype(jnp.float32), precision=lax.Precision.HIGHEST
    ).astype(jnp.bfloat16)
    return (mixed, grad_tokens, grad_gate[None], grad_up[None], grad_down[None])


def solution(mesh):
    return jax.shard_map(
        body,
        mesh=mesh,
        in_specs=(
            P(("dp", "expert", "tensor"), None),
            P(("dp", "expert", "tensor"), None),
            P(("dp", "expert", "tensor"), None),
            P("expert", "dp", "tensor"),
            P("expert", "dp", "tensor"),
            P("expert", "tensor", "dp"),
            P(("dp", "expert", "tensor"), None),
        ),
        out_specs=(
            P(("dp", "expert", "tensor"), None),
            P(("dp", "expert", "tensor"), None),
            P("expert", "dp", "tensor"),
            P("expert", "dp", "tensor"),
            P("expert", "tensor", "dp"),
        ),
        check_vma=False,
    )
```

```python
import functools

import jax
import jax.numpy as jnp
from jax import lax
from jax.experimental import pallas as pl
from jax.experimental.pallas import tpu as pltpu
from jax.sharding import PartitionSpec as P

MESH = pl.DeviceIdType.MESH


def remote(src, dst, send_sem, recv_sem, device):
    return pltpu.make_async_remote_copy(
        src_ref=src,
        dst_ref=dst,
        send_sem=send_sem,
        recv_sem=recv_sem,
        device_id=device,
        device_id_type=MESH,
    )


def dispatch_kernel(n_dp, n_exp, n_t, send_ref, out_ref, s1, r1, s2, r2, s3, own_sem):
    d, e, t = lax.axis_index("dp"), lax.axis_index("expert"), lax.axis_index("tensor")
    width = out_ref.shape[3]
    core = lax.rem(t, 2)
    mate = t + 1 - 2 * core
    offsets = [(dd, de) for dd in range(n_dp) for de in range(n_exp)]
    offsets = offsets[1:] + offsets[:1]
    peers = [lax.rem(t + 2 * k, n_t) for k in range(1, n_t // 2)]

    def at(dp, expert, tensor):
        return (dp, expert, tensor)

    barrier = pltpu.get_barrier_semaphore()
    for dd, de in offsets[:-1]:
        pl.semaphore_signal(
            barrier,
            inc=1,
            device_id=at(lax.rem(d + dd, n_dp), lax.rem(e + de, n_exp), t),
            device_id_type=MESH,
        )
    for peer in peers + [mate]:
        pl.semaphore_signal(barrier, inc=1, device_id=at(d, e, peer), device_id_type=MESH)
    pl.semaphore_wait(barrier, len(offsets) - 1 + len(peers) + 1)

    mine = e * n_dp + d
    first = []
    for k, (dd, de) in enumerate(offsets):
        dp_to, exp_to = lax.rem(d + dd, n_dp), lax.rem(e + de, n_exp)
        block = send_ref.at[exp_to, :, pl.ds(pl.multiple_of(dp_to * width, 128), width)]
        if k == len(offsets) - 1:
            own = pltpu.make_async_copy(block, out_ref.at[t, mine], own_sem)
            own.start()
        else:
            copy = remote(block, out_ref.at[t, mine], s1.at[k], r1.at[k], at(dp_to, exp_to, t))
            copy.start()
            first.append(copy)
    second = []
    order = [len(offsets) - 1] + list(range(len(offsets) - 1))
    for k in order:
        dd, de = offsets[k]
        source = lax.rem(e + n_exp - de, n_exp) * n_dp + lax.rem(d + n_dp - dd, n_dp)
        if k == len(offsets) - 1:
            own.wait()
        else:
            remote(
                out_ref.at[t, source], out_ref.at[t, source], s1.at[k], r1.at[k], at(d, e, mate)
            ).wait_recv()
        for j, peer in enumerate(peers + [mate]):
            copy = remote(
                out_ref.at[t, source],
                out_ref.at[t, source],
                s2.at[j, k],
                r2.at[j, k],
                at(d, e, peer),
            )
            copy.start()
            second.append(copy)
    third = []
    for k in order:
        dd, de = offsets[k]
        source = lax.rem(e + n_exp - de, n_exp) * n_dp + lax.rem(d + n_dp - dd, n_dp)
        for j in range(len(peers)):
            origin = lax.rem(t + n_t - 2 * (j + 1), n_t)
            block = out_ref.at[origin, source]
            remote(block, block, s2.at[j, k], r2.at[j, k], at(d, e, mate)).wait_recv()
            copy = remote(block, block, s3.at[j, k], r2.at[len(peers) + 1 + j, k], at(d, e, mate))
            copy.start()
            third.append(copy)
    for k in order:
        dd, de = offsets[k]
        source = lax.rem(e + n_exp - de, n_exp) * n_dp + lax.rem(d + n_dp - dd, n_dp)
        block = out_ref.at[mate, source]
        remote(
            block, block, s2.at[len(peers), k], r2.at[len(peers), k], at(d, e, mate)
        ).wait_recv()
        for j in range(len(peers)):
            block = out_ref.at[lax.rem(mate + n_t - 2 * (j + 1), n_t), source]
            remote(
                block, block, s3.at[j, k], r2.at[len(peers) + 1 + j, k], at(d, e, mate)
            ).wait_recv()
    for copy in first + second + third:
        copy.wait_send()


def dispatch(send, n_dp, n_exp, n_t):
    rows, model = send.shape[1], send.shape[2]
    sources = n_dp * n_exp
    peers = n_t // 2 - 1
    return pl.pallas_call(
        functools.partial(dispatch_kernel, n_dp, n_exp, n_t),
        out_shape=jax.ShapeDtypeStruct((n_t, sources, rows, model // n_dp), jnp.bfloat16),
        in_specs=[pl.BlockSpec(memory_space=pltpu.VMEM)],
        out_specs=pl.BlockSpec(memory_space=pltpu.VMEM),
        scratch_shapes=[
            pltpu.SemaphoreType.DMA((sources,)),
            pltpu.SemaphoreType.DMA((sources,)),
            pltpu.SemaphoreType.DMA((peers + 1, sources)),
            pltpu.SemaphoreType.DMA((2 * peers + 1, sources)),
            pltpu.SemaphoreType.DMA((peers, sources)),
            pltpu.SemaphoreType.DMA,
        ],
        compiler_params=pltpu.CompilerParams(
            collective_id=0, has_side_effects=True, vmem_limit_bytes=32 * 1024 * 1024
        ),
        name="dispatch",
    )(send)


LAG = 2


def chain_kernel(
    n, x_ref, g_ref, wg_ref, wu_ref, wd_ref, act_ref, part_ref,
    vgu, vd, part, rbuf, sbuf, out_acc, dx_acc, wsem, rs_s, rs_r, ag_s, ag_r
):
    d, e, t = lax.axis_index("dp"), lax.axis_index("expert"), lax.axis_index("tensor")
    n_chunks, hc = vd.shape[0], vd.shape[1]
    half = x_ref.shape[0] // 2

    @pl.when(d > 0)
    def _():
        pl.semaphore_signal(
            pltpu.get_barrier_semaphore(), inc=1, device_id=(d - 1, e, t), device_id_type=MESH
        )

    @pl.when(d < n - 1)
    def _():
        pl.semaphore_signal(
            pltpu.get_barrier_semaphore(), inc=1, device_id=(d + 1, e, t), device_id_type=MESH
        )

    def loads(c):
        cols = pl.ds(pl.multiple_of(c * hc, 128), hc)
        return (
            pltpu.make_async_copy(wg_ref.at[:, cols], vgu.at[c, :, pl.ds(0, hc)], wsem.at[0, c]),
            pltpu.make_async_copy(wu_ref.at[:, cols], vgu.at[c, :, pl.ds(hc, hc)], wsem.at[1, c]),
            pltpu.make_async_copy(wd_ref.at[cols, :], vd.at[c], wsem.at[2, c]),
        )

    @pl.loop(0, n_chunks)
    def _(c):
        for copy in loads(c):
            copy.start()

    @pl.when((d > 0) & (d < n - 1))
    def _():
        pl.semaphore_wait(pltpu.get_barrier_semaphore(), 2)

    @pl.when((d == 0) | (d == n - 1))
    def _():
        pl.semaphore_wait(pltpu.get_barrier_semaphore(), 1)

    def chain(s):
        return (d, d - 1, d + 1) if s == 0 else (n - 1 - d, d + 1, d - 1)

    def window(s, c):
        return act_ref.at[:, pl.ds(s * half, half), pl.ds(pl.multiple_of(c * hc, 128), hc)]

    def up_copy(s, c):
        up = chain(s)[1]
        return remote(sbuf.at[s, c], rbuf.at[s, c], rs_s.at[s, c], rs_r.at[s, c], (up, e, t))

    def down_copy(s, c):
        down = chain(s)[2]
        return remote(window(s, c), window(s, c), ag_s.at[s, c], ag_r.at[s, c], (down, e, t))

    def spread_step(s, i):
        p = chain(s)[0]
        c = i - LAG * (n - 1) - LAG * p

        @pl.when((p > 0) & (c >= 0) & (c < n_chunks))
        def _():
            down_copy(s, c).wait_recv()

            @pl.when(p < n - 1)
            def _():
                down_copy(s, c).start()

    def sum_step(s, i):
        p = chain(s)[0]
        c = i - LAG * (n - 1 - p)

        @pl.when((c >= 0) & (c < n_chunks))
        def _():
            rows = pl.ds(s * half, half)

            @pl.when(p < n - 1)
            def _():
                up_copy(s, c).wait_recv()
                part[c, rows, :] += rbuf[s, c].astype(jnp.float32)

            @pl.when(p > 0)
            def _():
                sbuf[s, c] = part[c, rows, :].astype(jnp.bfloat16)
                up_copy(s, c).start()

            @pl.when(p == 0)
            def _():
                gate = part[c, rows, pl.ds(0, hc)]
                upper = part[c, rows, pl.ds(hc, hc)]
                dhidden = part[c, rows, pl.ds(2 * hc, hc)]
                sigma = jax.nn.sigmoid(gate)
                active = gate * sigma
                cols = pl.ds(pl.multiple_of(c * hc, 128), hc)
                act_ref[0, rows, cols] = (active * upper).astype(jnp.bfloat16)
                act_ref[1, rows, cols] = (
                    dhidden * upper * sigma * (1.0 + gate * (1.0 - sigma))
                ).astype(jnp.bfloat16)
                act_ref[2, rows, cols] = (dhidden * active).astype(jnp.bfloat16)
                down_copy(s, c).start()

    def output_step(c):
        cols = pl.ds(pl.multiple_of(c * hc, 128), hc)
        out_acc[...] += jnp.dot(
            act_ref[0, :, cols], vd[c], preferred_element_type=jnp.float32
        )
        both = jnp.concatenate([act_ref[1, :, cols], act_ref[2, :, cols]], axis=1)
        dx_acc[...] += lax.dot_general(
            both, vgu[c], (((1,), (1,)), ((), ())), preferred_element_type=jnp.float32
        )

    out_acc[...] = jnp.zeros_like(out_acc)
    dx_acc[...] = jnp.zeros_like(dx_acc)

    @pl.loop(0, n_chunks + 2 * LAG * (n - 1))
    def _(i):
        @pl.when(i < n_chunks)
        def _():
            for copy in loads(i):
                copy.wait()
            part[i, :, pl.ds(0, 2 * hc)] = jnp.dot(
                x_ref[...], vgu[i], preferred_element_type=jnp.float32
            )
            part[i, :, pl.ds(2 * hc, hc)] = lax.dot_general(
                g_ref[...], vd[i], (((1,), (1,)), ((), ())), preferred_element_type=jnp.float32
            )

        for s in range(2):
            spread_step(s, i)
        for s in range(2):
            sum_step(s, i)

        @pl.when(i >= 2 * LAG * (n - 1))
        def _():
            output_step(i - 2 * LAG * (n - 1))

    cap = part_ref.shape[1] // 2

    @pl.loop(0, part_ref.shape[0])
    def _(b):
        rows = pl.ds(pl.multiple_of(b * cap, 8), cap)
        part_ref[b] = jnp.concatenate([out_acc[rows, :], dx_acc[rows, :]], axis=0).astype(
            jnp.bfloat16
        )

    @pl.loop(0, n_chunks)
    def _(c):
        for s in range(2):
            p = chain(s)[0]

            @pl.when(p > 0)
            def _():
                up_copy(s, c).wait_send()

            @pl.when(p < n - 1)
            def _():
                down_copy(s, c).wait_send()


def hidden_grads(x, g, wg, wu, wd, n_dp, cap):
    rows, quarter = x.shape
    hidden = wg.shape[1]
    hc = 128
    nc = hidden // hc
    vmem = pl.BlockSpec(memory_space=pltpu.VMEM)
    anywhere = pl.BlockSpec(memory_space=pl.ANY)
    return pl.pallas_call(
        functools.partial(chain_kernel, n_dp),
        out_shape=(
            jax.ShapeDtypeStruct((3, rows, hidden), jnp.bfloat16),
            jax.ShapeDtypeStruct((rows // cap, 2 * cap, quarter), jnp.bfloat16),
        ),
        in_specs=[vmem, vmem, anywhere, anywhere, anywhere],
        out_specs=(vmem, vmem),
        scratch_shapes=[
            pltpu.VMEM((nc, quarter, 2 * hc), jnp.bfloat16),
            pltpu.VMEM((nc, hc, quarter), jnp.bfloat16),
            pltpu.VMEM((nc, rows, 3 * hc), jnp.float32),
            pltpu.VMEM((2, nc, rows // 2, 3 * hc), jnp.bfloat16),
            pltpu.VMEM((2, nc, rows // 2, 3 * hc), jnp.bfloat16),
            pltpu.VMEM((rows, quarter), jnp.float32),
            pltpu.VMEM((rows, quarter), jnp.float32),
            pltpu.SemaphoreType.DMA((3, nc)),
            pltpu.SemaphoreType.DMA((2, nc)),
            pltpu.SemaphoreType.DMA((2, nc)),
            pltpu.SemaphoreType.DMA((2, nc)),
            pltpu.SemaphoreType.DMA((2, nc)),
        ],
        compiler_params=pltpu.CompilerParams(
            collective_id=1, has_side_effects=True, vmem_limit_bytes=54 * 1024 * 1024
        ),
        name="chain",
    )(x, g, wg, wu, wd)


def collect_kernel(
    n_dp, n_exp, n_t, part_ref, home_ref, in_a, pair, in_b, total, a_s, a_r, b_s, b_r, c_s, c_r
):
    d, e, t = lax.axis_index("dp"), lax.axis_index("expert"), lax.axis_index("tensor")
    width = part_ref.shape[3]
    core = lax.rem(t, 2)
    mate = t + 1 - 2 * core
    n_hi = n_t // 2
    offsets = [(dd, de) for dd in range(n_dp) for de in range(n_exp)]
    offsets = offsets[1:] + offsets[:1]
    last = len(offsets) - 1

    def source(k):
        dd, de = offsets[k]
        return lax.rem(e + de, n_exp) * n_dp + lax.rem(d + dd, n_dp)

    barrier = pltpu.get_barrier_semaphore()
    for dd, de in offsets[:-1]:
        pl.semaphore_signal(
            barrier,
            inc=1,
            device_id=(lax.rem(d + dd, n_dp), lax.rem(e + de, n_exp), t),
            device_id_type=MESH,
        )
    for peer in [lax.rem(t + 2 * j, n_t) for j in range(1, n_hi)] + [mate]:
        pl.semaphore_signal(barrier, inc=1, device_id=(d, e, peer), device_id_type=MESH)
    pl.semaphore_wait(barrier, last + n_hi)

    order = list(range(1, n_hi)) + [0]
    swaps = {}
    for j in order:
        swaps[j] = remote(
            part_ref.at[lax.rem(mate + 2 * j, n_t)],
            in_a.at[j],
            a_s.at[j],
            a_r.at[j],
            (d, e, mate),
        )
        swaps[j].start()
    sums = []
    for j in order[:-1]:
        swaps[j].wait_recv()
        peer = lax.rem(t + 2 * j, n_t)
        for k in range(last + 1):
            where = source(k)
            pair[j - 1, k] = (
                part_ref[peer, where].astype(jnp.float32) + in_a[j, where].astype(jnp.float32)
            ).astype(jnp.bfloat16)
            copy = remote(
                pair.at[j - 1, k],
                in_b.at[j - 1, k],
                b_s.at[j - 1, k],
                b_r.at[j - 1, k],
                (d, e, peer),
            )
            copy.start()
            sums.append(copy)
    swaps[0].wait_recv()
    homes = []
    for k in range(last + 1):
        where = source(k)
        value = part_ref[t, where].astype(jnp.float32) + in_a[0, where].astype(jnp.float32)
        for j in order[:-1]:
            sums[(j - 1) * (last + 1) + k].wait_recv()
            value = value + in_b[j - 1, k].astype(jnp.float32)
        columns = pl.ds(pl.multiple_of(d * width, 128), width)
        if k == last:
            home_ref[e, :, columns] = value.astype(jnp.bfloat16)
        else:
            total[k] = value.astype(jnp.bfloat16)
            dd, de = offsets[k]
            copy = remote(
                total.at[k],
                home_ref.at[e, :, columns],
                c_s.at[k],
                c_r.at[k],
                (lax.rem(d + dd, n_dp), lax.rem(e + de, n_exp), t),
            )
            copy.start()
            homes.append(copy)
    for k in range(last):
        dd, de = offsets[k]
        from_dp, from_exp = lax.rem(d + n_dp - dd, n_dp), lax.rem(e + n_exp - de, n_exp)
        columns = pl.ds(pl.multiple_of(from_dp * width, 128), width)
        remote(
            total.at[k], home_ref.at[from_exp, :, columns], c_s.at[k], c_r.at[k], (d, e, mate)
        ).wait_recv()
    for copy in list(swaps.values()) + sums + homes:
        copy.wait_send()


def collect(part, n_dp, n_exp, n_t):
    rows, width = part.shape[2], part.shape[3]
    sources, n_hi = n_dp * n_exp, n_t // 2
    vmem = pl.BlockSpec(memory_space=pltpu.VMEM)
    return pl.pallas_call(
        functools.partial(collect_kernel, n_dp, n_exp, n_t),
        out_shape=jax.ShapeDtypeStruct((n_exp, rows, n_dp * width), jnp.bfloat16),
        in_specs=[vmem],
        out_specs=vmem,
        scratch_shapes=[
            pltpu.VMEM((n_hi, sources, rows, width), jnp.bfloat16),
            pltpu.VMEM((n_hi - 1, sources, rows, width), jnp.bfloat16),
            pltpu.VMEM((n_hi - 1, sources, rows, width), jnp.bfloat16),
            pltpu.VMEM((sources - 1, rows, width), jnp.bfloat16),
            pltpu.SemaphoreType.DMA((n_hi,)),
            pltpu.SemaphoreType.DMA((n_hi,)),
            pltpu.SemaphoreType.DMA((n_hi - 1, sources)),
            pltpu.SemaphoreType.DMA((n_hi - 1, sources)),
            pltpu.SemaphoreType.DMA((sources - 1,)),
            pltpu.SemaphoreType.DMA((sources - 1,)),
        ],
        compiler_params=pltpu.CompilerParams(
            collective_id=2, has_side_effects=True, vmem_limit_bytes=32 * 1024 * 1024
        ),
        name="collect",
    )(part)


def grads_kernel(n, left_ref, *refs):
    for right_ref, out_ref in zip(refs[:n], refs[n:]):
        out_ref[...] = lax.dot_general(
            left_ref[...],
            right_ref[...],
            (((0,), (0,)), ((), ())),
            preferred_element_type=jnp.float32,
        )


def weight_grads(left, rights):
    depth, rows = left.shape
    columns = rights[0].shape[1]
    tile = 256
    n = len(rights)
    whole = pl.BlockSpec((depth, columns), lambda i: (0, 0))
    return pl.pallas_call(
        functools.partial(grads_kernel, n),
        grid=(rows // tile,),
        out_shape=[jax.ShapeDtypeStruct((rows, columns), jnp.float32)] * n,
        in_specs=[pl.BlockSpec((depth, tile), lambda i: (0, i))] + [whole] * n,
        out_specs=[pl.BlockSpec((tile, columns), lambda i: (i, 0))] * n,
        compiler_params=pltpu.CompilerParams(vmem_limit_bytes=40 * 1024 * 1024),
        cost_estimate=pl.CostEstimate(
            flops=2 * n * depth * rows * columns,
            bytes_accessed=4 * n * rows * columns,
            transcendentals=0,
        ),
        name="weight_grads",
    )(left, *rights)


def body(tokens, expert_ids, gate_values, w_gate, w_up, w_down, grad_out):
    tok_rows = tokens.shape[0]
    cap = tok_rows // 2
    n_exp = lax.axis_size("expert")
    gate_mat = w_gate[0]
    up_mat = w_up[0]
    down_mat = w_down[0]
    slots = jnp.arange(cap, dtype=jnp.int32)
    selector_list = []
    weight_list = []
    for expert in range(n_exp):
        chosen = (expert_ids == expert).astype(jnp.int32)
        flat_chosen = chosen.reshape(-1)
        ranks = jnp.cumsum(flat_chosen) - 1
        onehot = ((ranks[:, None] == slots[None, :]) & (flat_chosen[:, None] > 0)).astype(
            jnp.float32
        )
        selector_list.append(jnp.sum(onehot.reshape(tok_rows, 2, cap), axis=1).T)
        weight_list.append(jnp.sum(gate_values * chosen.astype(jnp.float32), axis=1))
    selector = jnp.stack(selector_list)
    weights = jnp.stack(weight_list)
    selector_bf = selector.astype(jnp.bfloat16)
    send_rows = jnp.einsum(
        "wct,td->wcd", selector_bf, tokens, preferred_element_type=jnp.float32
    ).astype(jnp.bfloat16)
    scaled = (weights[:, :, None] * grad_out.astype(jnp.float32)[None]).astype(jnp.bfloat16)
    send_grads = jnp.einsum(
        "wct,wtd->wcd", selector_bf, scaled, preferred_element_type=jnp.float32
    ).astype(jnp.bfloat16)
    n_dp, n_t = lax.axis_size("dp"), lax.axis_size("tensor")
    panels = dispatch(jnp.concatenate([send_rows, send_grads], axis=1), n_dp, n_exp, n_t)
    quarter = panels.shape[3]
    panel_rows = panels[:, :, :cap].reshape(-1, quarter)
    grad_panels = panels[:, :, cap:].reshape(-1, quarter)

    acts, part = hidden_grads(panel_rows, grad_panels, gate_mat, up_mat, down_mat, n_dp, cap)
    hidden_all, dgate_all, dup_all = acts
    home = collect(part.reshape(panels.shape), n_dp, n_exp, n_t)
    out_home, back_home = home[:, :cap], home[:, cap:]
    weighted = selector * weights[:, None, :]
    mixed = jnp.einsum(
        "wct,wcd->td", weighted, out_home.astype(jnp.float32), precision=lax.Precision.HIGHEST
    ).astype(jnp.bfloat16)
    (grad_down,) = weight_grads(hidden_all, [grad_panels])
    grad_gate, grad_up = weight_grads(panel_rows, [dgate_all, dup_all])
    grad_tokens = jnp.einsum(
        "wct,wcd->td", selector, back_home.astype(jnp.float32), precision=lax.Precision.HIGHEST
    ).astype(jnp.bfloat16)
    return (mixed, grad_tokens, grad_gate[None], grad_up[None], grad_down[None])


def solution(mesh):
    return jax.shard_map(
        body,
        mesh=mesh,
        in_specs=(
            P(("dp", "expert", "tensor"), None),
            P(("dp", "expert", "tensor"), None),
            P(("dp", "expert", "tensor"), None),
            P("expert", "dp", "tensor"),
            P("expert", "dp", "tensor"),
            P("expert", "tensor", "dp"),
            P(("dp", "expert", "tensor"), None),
        ),
        out_specs=(
            P(("dp", "expert", "tensor"), None),
            P(("dp", "expert", "tensor"), None),
            P("expert", "dp", "tensor"),
            P("expert", "dp", "tensor"),
            P("expert", "tensor", "dp"),
        ),
        check_vma=False,
    )
```
